32 devices in a mesh: leaf: 32 (over z, y, x, core).
Axes of the slice: x: 2, y: 2, z: 4, core: 2. Of those that a mesh axis runs over, the one named last changes fastest.
Arguments:
- right_side: float32 [16, 131072], P(None, 'leaf'), may hold values from -12 to 12
- basis: bfloat16 [512, 64, 256], P('leaf'), may hold values from -0.5 to 0.5
- transfer: bfloat16 [960, 64, 64], P('leaf'), may hold values from -0.5 to 0.5
- near_tiles: bfloat16 [512, 8, 256, 256], P('leaf'), may hold values from -4 to 4
- near_source: int32 [512, 8], P('leaf'), may hold values from 0 to 511, as said below
- near_count: int32 [512], P('leaf'), may hold values from 1 to 8, as said below
- couple: bfloat16 [448, 6, 64, 64], P('leaf'), may hold values from -1.5 to 1.5
- couple_source: int32 [448, 6], P('leaf'), may hold values from 0 to 255, as said below
- couple_count: int32 [448], P('leaf'), may hold values from 1 to 6, as said below
- root_couple: bfloat16 [32, 5, 64, 64], P('leaf'), may hold values from -4 to 4
- root_mask: int32 [32, 5], P('leaf'), may hold values 0 or 1
Outputs:
- solution: float32 [16, 131072], P(None, 'leaf')
- residual: float32 [16, 131072], P(None, 'leaf')
The draws below stay inside these ranges and needn't reach their ends.
Inputs may be any that keep to these rules, and one draw needn't show every extreme that they name: `near_source`: slot 0 of leaf g is g itself; every slot names a different leaf of the same subtree or of one of the two subtrees beside it. `near_count`: the live tiles are the first slots; on each subtree some leaf has the most live tiles of that subtree. `couple_source`: a source is a cluster of the same level, not the cluster itself, in the same subtree or in one of the two subtrees beside it. `couple_count`: the live blocks are the first slots.
All inputs are finite; a program needn't handle non-finite values. No bound on the sum of `root_mask` on one device may be relied on, other than what follows from the above.
Results may differ from the reference program's by a relative error of at most 0.014.
Values may be sent and summed in bfloat16 or wider, within the bound.
A program may use at most 128 MiB of HBM per device.

```python
import jax
import jax.numpy as jnp
import numpy as np
from jax import lax

LEAF = 256
RANK = 64
NRHS = 16
NEAR = 8
COUPLE = 6
ROOT_BITS = 5
ITERS = 2
LEAF_DEV = 16
NLEAF = 512
NPTS = 131072
NLOC = 448
NTRANS = 960
N_LEAF = 32


def draw_right_side(key, part):
    key = jax.random.fold_in(key, 5)
    place = jnp.arange(NPTS, dtype=jnp.float32) / NPTS
    scale = 1.0 + 2.0 * place
    base = jnp.clip(jax.random.normal(key, (NRHS, NPTS), jnp.float32), -4.0, 4.0)
    return (base * scale[None, :]).astype(jnp.float32)


def draw_near_tiles(key, part):
    key = jax.random.fold_in(key, 31)
    shape = (NLEAF, NEAR, LEAF, LEAF)
    base = jnp.clip(jax.random.normal(key, shape, jnp.float32), -4.0, 4.0)
    base = base * LEAF ** (-0.5)
    slot_ids = lax.broadcasted_iota(jnp.int32, shape, 1)
    rows = lax.broadcasted_iota(jnp.int32, shape, 2)
    cols = lax.broadcasted_iota(jnp.int32, shape, 3)
    diagonal = jnp.where((slot_ids == 0) & (rows == cols), 3.0, 0.0).astype(jnp.float32)
    return (base + diagonal).astype(jnp.bfloat16)


def draw_near_source(key, part):
    key = jax.random.fold_in(key, 11)
    first, second = jax.random.split(key)
    span = 3 * LEAF_DEV
    leaf_ids = jnp.arange(NLEAF, dtype=jnp.int32)
    device = leaf_ids // LEAF_DEV
    beside = jnp.where(device > 0, device - 1, device + 1)
    forced = beside * LEAF_DEV + jax.random.randint(first, (NLEAF,), 0, LEAF_DEV, dtype=jnp.int32)
    offsets = jnp.arange(span, dtype=jnp.int32) - LEAF_DEV
    candidate = (device * LEAF_DEV)[:, None] + offsets[None, :]
    usable = (candidate >= 0) & (candidate < NLEAF) & (candidate != leaf_ids[:, None]) & (candidate != forced[:, None])
    scores = jax.random.randint(second, (NLEAF, span), 0, 2 ** 20, dtype=jnp.int32) * span + jnp.arange(span, dtype=jnp.int32)[None, :]
    scores = jnp.where(usable, scores, -1)
    unused, picked = lax.top_k(scores, NEAR - 2)
    others = jnp.take_along_axis(candidate, picked, axis=1)
    return jnp.concatenate([leaf_ids[:, None], forced[:, None], others], axis=1).astype(jnp.int32)


def draw_near_count(key, part):
    key = jax.random.fold_in(key, 12)
    first, second, third, fourth = jax.random.split(key, 4)
    subtrees = NLEAF // LEAF_DEV
    most = jax.random.randint(first, (subtrees,), (NEAR + 1) // 2, NEAR + 1, dtype=jnp.int32)
    heavy = jax.random.randint(second, (), 0, subtrees, dtype=jnp.int32)
    most = jnp.where(jnp.arange(subtrees, dtype=jnp.int32) == heavy, NEAR, most)
    counts = jax.random.randint(third, (subtrees, LEAF_DEV), 1, NEAR + 1, dtype=jnp.int32)
    counts = jnp.minimum(counts, most[:, None])
    chosen = jax.random.randint(fourth, (subtrees,), 0, LEAF_DEV, dtype=jnp.int32)
    counts = jnp.where(jnp.arange(LEAF_DEV, dtype=jnp.int32)[None, :] == chosen[:, None], most[:, None], counts)
    return counts.reshape(NLEAF).astype(jnp.int32)


def draw_couple_source(key, part):
    key = jax.random.fold_in(key, 21)
    first, second = jax.random.split(key)
    per = LEAF_DEV - 2
    subtrees = NLOC // per
    widths = []
    places = []
    width = LEAF_DEV // 2
    while width > 1:
        widths += [width] * width
        places += list(range(width))
        width //= 2
    width_table = jnp.array(np.array(widths, np.int32))
    place_table = jnp.array(np.array(places, np.int32))
    row = jnp.arange(NLOC, dtype=jnp.int32)
    device = row // per
    offset = row % per
    count = width_table[offset]
    itself = device * count + place_table[offset]
    low = jnp.maximum(device - 1, 0) * count
    high = jnp.minimum(device + 2, subtrees) * count
    picked = jax.random.randint(first, (NLOC, COUPLE), low[:, None], high[:, None] - 1, dtype=jnp.int32)
    picked = jnp.where(picked >= itself[:, None], picked + 1, picked)
    beside = jnp.where(device > 0, device - 1, device + 1)
    forced = beside * count + jax.random.randint(second, (NLOC,), 0, count, dtype=jnp.int32)
    picked = picked.at[:, 0].set(forced)
    return picked.astype(jnp.int32)


def draw_couple_count(key, part):
    key = jax.random.fold_in(key, 22)
    first, second = jax.random.split(key)
    counts = jax.random.randint(first, (NLOC,), 1, COUPLE + 1, dtype=jnp.int32)
    fullest = jax.random.randint(second, (), 0, NLOC, dtype=jnp.int32)
    return jnp.where(jnp.arange(NLOC, dtype=jnp.int32) == fullest, COUPLE, counts).astype(jnp.int32)


def with_ends(drawn, key, low, top_value):
    index_at = [jax.random.randint(jax.random.fold_in(key, axis), (), 0, length) for axis, length in enumerate(drawn.shape)]
    main_axis = drawn.shape.index(max(drawn.shape))
    next_to = index_at[:main_axis] + [(index_at[main_axis] + 1) % drawn.shape[main_axis]] + index_at[main_axis + 1:]
    return drawn.at[tuple(index_at)].set(low).at[tuple(next_to)].set(top_value)


def level_of(own_key, extent, cuts, smallest, top_value):
    factor_of, own = 1.0, jax.random.fold_in(own_key, 6)
    for axis_at, parts in cuts:
        heights = jnp.exp(jax.random.uniform(jax.random.fold_in(own, axis_at), (parts,), jnp.float32, smallest / len(cuts), top_value / len(cuts)))
        factor_of = factor_of * jnp.repeat(heights, extent[axis_at] // parts).reshape([-1 if axis == axis_at else 1 for axis in range(len(extent))])
    return factor_of


def noise(own_key, extent, spread, bound, cuts=(), kind=jnp.bfloat16):
    loudness = level_of(own_key, extent, cuts, -0.22, 0.18) if cuts else 1.0
    drawn = jax.random.normal(own_key, extent, jnp.float32) * spread * loudness
    return jnp.minimum(jnp.maximum(drawn, -bound), bound).astype(kind)


def setup_inputs(seed: int = 0) -> dict:
    seeds = jax.random.split(jax.random.key(seed), 12)
    return {
        "right_side": draw_right_side(jax.random.fold_in(seeds[11], 71), 0),
        "basis": noise(seeds[1], (NLEAF, RANK, LEAF), (LEAF // 2) ** -0.5, 0.5, ((0, 32),)),
        "transfer": noise(seeds[2], (NTRANS, RANK, RANK), (2 * RANK) ** -0.5, 0.5, ((0, 32),)),
        "near_tiles": draw_near_tiles(jax.random.fold_in(seeds[11], 71), 0),
        "near_source": draw_near_source(jax.random.fold_in(seeds[11], 71), 0),
        "near_count": draw_near_count(jax.random.fold_in(seeds[11], 71), 0),
        "couple": noise(seeds[6], (NLOC, COUPLE, RANK, RANK), (RANK // 4) ** -0.5, 1.5, ((0, 32),)),
        "couple_source": draw_couple_source(jax.random.fold_in(seeds[11], 71), 0),
        "couple_count": draw_couple_count(jax.random.fold_in(seeds[11], 71), 0),
        "root_couple": noise(seeds[9], (N_LEAF, ROOT_BITS, RANK, RANK), 2 ** -0.5, 4.0, ((0, 32),)),
        "root_mask": with_ends((jax.random.randint(seeds[10], (N_LEAF, ROOT_BITS), 0, 4) < 3).astype(jnp.int32), jax.random.fold_in(seeds[10], 1), 0, 1),
    }


def level_sizes(leaf_dev):
    sizes = [leaf_dev]
    while sizes[-1] > 1:
        sizes.append(sizes[-1] // 2)
    return sizes


def split_levels(stacked, first, last, sizes, devices):
    rows = stacked.reshape((devices, -1) + stacked.shape[1:])
    pieces = []
    start = 0
    for level in range(first, last):
        part = rows[:, start:start + sizes[level]]
        pieces.append(part.reshape((devices * sizes[level],) + stacked.shape[1:]))
        start += sizes[level]
    return pieces


def apply_matrix(vector, basis, transfer, near_tiles, near_source, near_count, couple, couple_source, couple_count, root_couple, root_mask):
    f32 = jnp.float32
    sizes = level_sizes(LEAF_DEV)
    top = len(sizes) - 1
    operand = vector.astype(jnp.bfloat16)
    leaves = operand.reshape(NRHS, NLEAF, LEAF).transpose(1, 0, 2)
    basis_f = basis.astype(f32)
    coef = [jnp.einsum("knp,krp->knr", leaves.astype(f32), basis_f).astype(jnp.bfloat16)]
    lifts = split_levels(transfer, 0, top, sizes, N_LEAF)
    for level in range(1, top + 1):
        raised = jnp.einsum("knr,krs->kns", coef[level - 1].astype(f32), lifts[level - 1].astype(f32))
        coef.append(raised.reshape(-1, 2, NRHS, RANK).sum(axis=1).astype(jnp.bfloat16))
    roots = coef[top]
    device = jnp.arange(N_LEAF, dtype=jnp.int32)
    total = jnp.zeros((N_LEAF, NRHS, RANK), f32)
    for bit in range(ROOT_BITS):
        partner = jnp.bitwise_xor(device, 2 ** bit)
        term = jnp.einsum("knr,krs->kns", roots[partner].astype(f32), root_couple[:, bit].astype(f32))
        total = total + root_mask[:, bit].astype(f32)[:, None, None] * term
    field = total.astype(jnp.bfloat16)
    couplings = split_levels(couple, 1, top, sizes, N_LEAF)
    sources = split_levels(couple_source, 1, top, sizes, N_LEAF)
    counts = split_levels(couple_count, 1, top, sizes, N_LEAF)
    for level in range(top - 1, -1, -1):
        parent = jnp.repeat(field, 2, axis=0).astype(f32)
        down = jnp.einsum("kns,krs->knr", parent, lifts[level].astype(f32))
        if level >= 1:
            for slot in range(COUPLE):
                live = (slot < counts[level - 1]).astype(f32)[:, None, None]
                src = coef[level][sources[level - 1][:, slot]].astype(f32)
                down = down + live * jnp.einsum("knr,krs->kns", src, couplings[level - 1][:, slot].astype(f32))
        field = down.astype(jnp.bfloat16)
    far = jnp.einsum("knr,krp->knp", field.astype(f32), basis_f)

    def one_subtree(args):
        tiles, srcs, cnts = args
        acc = jnp.zeros((LEAF_DEV, NRHS, LEAF), f32)
        for slot in range(NEAR):
            live = (slot < cnts).astype(f32)[:, None, None]
            xs = leaves[srcs[:, slot]].astype(f32)
            acc = acc + live * jnp.einsum("knp,kpq->knq", xs, tiles[:, slot].astype(f32))
        return acc

    near = lax.map(one_subtree, (near_tiles.reshape(N_LEAF, LEAF_DEV, NEAR, LEAF, LEAF), near_source.reshape(N_LEAF, LEAF_DEV, NEAR), near_count.reshape(N_LEAF, LEAF_DEV)))
    near = near.reshape(NLEAF, NRHS, LEAF)
    return (far + near).transpose(1, 0, 2).reshape(NRHS, NPTS)


def reference(right_side, basis, transfer, near_tiles, near_source, near_count, couple, couple_source, couple_count, root_couple, root_mask):
    solution = jnp.zeros_like(right_side)
    residual = right_side
    for step in range(ITERS):
        image = apply_matrix(residual, basis, transfer, near_tiles, near_source, near_count, couple, couple_source, couple_count, root_couple, root_mask)
        upper = jnp.sum(residual * image, axis=1)
        lower = jnp.sum(image * image, axis=1) + 1e-6
        alpha = (upper / lower)[:, None]
        solution = solution + alpha * residual
        residual = residual - alpha * image
    return solution, residual
```

```python
import functools

import jax
import jax.numpy as jnp
from jax import lax
from jax.experimental import pallas as pl
from jax.experimental.pallas import tpu as pltpu
from jax.sharding import PartitionSpec as P

MESH = pl.DeviceIdType.MESH
F32 = jnp.float32
BF16 = jnp.bfloat16
SHRINK = 2.0**-10
GROW = 2.0**10
UNROLL = 4


def dot(a, b):
    return jnp.dot(a, b, preferred_element_type=F32)


def dot_t(a, b):
    return lax.dot_general(a, b, (((1,), (1,)), ((), ())), preferred_element_type=F32)


def level_sizes(leaf_dev):
    sizes = [leaf_dev]
    while sizes[-1] > 1:
        sizes.append(sizes[-1] // 2)
    return sizes


def kernel(
    count,
    near_source,
    near_count,
    couple_source,
    couple_count,
    root_mask,
    rhs_hbm,
    basis_hbm,
    transfer_hbm,
    near_hbm,
    couple_hbm,
    root_hbm,
    sol_ref,
    res_ref,
    rhs,
    basis,
    transfer,
    near,
    couple,
    root,
    image_a,
    image_b,
    field0,
    win_a,
    win_b,
    cwin_a,
    cwin_b,
    own_a,
    own_b,
    part_a,
    part_b,
    red_a,
    red_b,
    load_sem,
    near_sem,
    halo_send,
    halo_recv,
    coef_send,
    coef_recv,
    root_send,
    root_recv,
    red_send,
    red_recv,
):
    leaf_dev, rank, leaf = basis.shape
    slots = near.shape[1]
    nrhs = rhs.shape[0]
    bits = root.shape[0]
    sizes = level_sizes(leaf_dev)
    top = len(sizes) - 1
    starts = [sum(sizes[:level]) for level in range(top)]
    me = lax.axis_index("leaf")
    has_left = me > 0
    has_right = me < count - 1

    loads = [
        pltpu.make_async_copy(src, dst, load_sem.at[i])
        for i, (src, dst) in enumerate(
            (
                (rhs_hbm, rhs),
                (basis_hbm, basis),
                (transfer_hbm, transfer),
                (couple_hbm, couple),
                (root_hbm, root),
            )
        )
    ]
    for load in loads:
        load.start()

    def near_load(g):
        return pltpu.make_async_copy(near_hbm.at[g], near.at[g], near_sem.at[g])

    for g in range(leaf_dev):
        near_load(g).start()

    barrier = pltpu.get_barrier_semaphore()

    def greet(k, carry):
        pl.semaphore_signal(
            barrier, inc=1, device_id=(lax.rem(me + k, count),), device_id_type=MESH
        )
        return carry

    lax.fori_loop(1, count, greet, 0)

    def halo_copies(it, win):
        own = win.at[pl.ds(leaf_dev, leaf_dev)]
        to_right = pltpu.make_async_remote_copy(
            src_ref=own,
            dst_ref=win.at[pl.ds(0, leaf_dev)],
            send_sem=halo_send.at[it, 0],
            recv_sem=halo_recv.at[it, 0],
            device_id=(me + 1,),
            device_id_type=MESH,
        )
        to_left = pltpu.make_async_remote_copy(
            src_ref=own,
            dst_ref=win.at[pl.ds(2 * leaf_dev, leaf_dev)],
            send_sem=halo_send.at[it, 1],
            recv_sem=halo_recv.at[it, 1],
            device_id=(me - 1,),
            device_id_type=MESH,
        )
        return to_right, to_left

    def coef_copies(it, level, cwin):
        size = sizes[level]
        own = cwin.at[pl.ds(size, size)]
        to_right = pltpu.make_async_remote_copy(
            src_ref=own,
            dst_ref=cwin.at[pl.ds(0, size)],
            send_sem=coef_send.at[it, level - 1, 0],
            recv_sem=coef_recv.at[it, level - 1, 0],
            device_id=(me + 1,),
            device_id_type=MESH,
        )
        to_left = pltpu.make_async_remote_copy(
            src_ref=own,
            dst_ref=cwin.at[pl.ds(2 * size, size)],
            send_sem=coef_send.at[it, level - 1, 1],
            recv_sem=coef_recv.at[it, level - 1, 1],
            device_id=(me - 1,),
            device_id_type=MESH,
        )
        return to_right, to_left

    def start_pair(pair):
        to_right, to_left = pair

        @pl.when(has_right)
        def _():
            to_right.start()

        @pl.when(has_left)
        def _():
            to_left.start()

    def recv_pair(pair):
        to_right, to_left = pair

        @pl.when(has_left)
        def _():
            to_right.wait_recv()

        @pl.when(has_right)
        def _():
            to_left.wait_recv()

    def sent_pair(pair):
        to_right, to_left = pair

        @pl.when(has_right)
        def _():
            to_right.wait_send()

        @pl.when(has_left)
        def _():
            to_left.wait_send()

    def root_copy(it, bit, own):
        step = 1 << bit
        partner = me + step * (1 - 2 * lax.rem(me // step, 2))
        return pltpu.make_async_remote_copy(
            src_ref=own.at[0],
            dst_ref=own.at[1 + bit],
            send_sem=root_send.at[it, bit],
            recv_sem=root_recv.at[it, bit],
            device_id=(partner,),
            device_id_type=MESH,
        )

    def upward(it, win, cwins, own):
        coef = [
            dot_t(win[leaf_dev + g], basis[g]).astype(BF16) for g in range(leaf_dev)
        ]
        for level in range(1, top + 1):
            at = starts[level - 1]
            raised = []
            for j in range(sizes[level]):
                raised.append(
                    (
                        dot(coef[2 * j], transfer[at + 2 * j])
                        + dot(coef[2 * j + 1], transfer[at + 2 * j + 1])
                    ).astype(BF16)
                )
            coef = raised
            if level < top:
                cwin = cwins[level - 1]
                for j in range(sizes[level]):
                    cwin[sizes[level] + j] = coef[j]
                start_pair(coef_copies(it, level, cwin))
        own[0] = coef[0]
        for bit in range(bits):
            root_copy(it, bit, own).start()

    def downward(it, cwins, own):
        for level in range(1, top):
            recv_pair(coef_copies(it, level, cwins[level - 1]))
        for bit in range(bits):
            root_copy(it, bit, own).wait_recv()
        total = jnp.zeros((nrhs, rank), F32)
        for bit in range(bits):
            total = total + root_mask[0, bit].astype(F32) * dot(own[1 + bit], root[bit])
        field = [total.astype(BF16)]
        for level in range(top - 1, -1, -1):
            down = []
            for j in range(sizes[level]):
                value = dot_t(field[j // 2], transfer[starts[level] + j])
                if level >= 1:
                    row = starts[level] - sizes[0] + j
                    live_slots = couple_count[row]
                    for s in range(couple.shape[1]):
                        index = couple_source[s, row] - (me - 1) * sizes[level]
                        index = jnp.clip(index, 0, 3 * sizes[level] - 1)
                        live = (s < live_slots).astype(F32)
                        value = value + live * dot(
                            cwins[level - 1][index], couple[row, s]
                        )
                down.append(value.astype(BF16))
            field = down
        for g in range(leaf_dev):
            field0[g] = field[g]

    def leaves(it, win, image, wait):
        base = (me - 1) * leaf_dev

        def step(i, carry):
            if wait:
                for u in range(UNROLL):
                    near_load(i * UNROLL + u).wait()
            for u in range(UNROLL):
                g = i * UNROLL + u
                live_slots = near_count[g]
                picked = []
                for s in range(slots):
                    live = (s < live_slots).astype(F32).astype(BF16)
                    index = jnp.clip(near_source[s, g] - base, 0, 3 * leaf_dev - 1)
                    picked.append(win[index] * live)
                x = jnp.concatenate(picked, axis=1)
                tile = near[g].reshape(slots * leaf, leaf)
                block = dot(x, tile) + dot(field0[g], basis[g])
                image[:, pl.ds(pl.multiple_of(g * leaf, leaf), leaf)] = block
            return carry

        lax.fori_loop(0, leaf_dev // UNROLL, step, 0)

    rows = lax.broadcasted_iota(jnp.int32, (nrhs, 128), 0)
    lanes = lax.broadcasted_iota(jnp.int32, (nrhs, 128), 1)

    def red_copy(it, k, part, red):
        return pltpu.make_async_remote_copy(
            src_ref=part,
            dst_ref=red.at[me],
            send_sem=red_send.at[it, k],
            recv_sem=red_recv.at[it, k],
            device_id=(lax.rem(me + k, count),),
            device_id_type=MESH,
        )

    def reduce_start(it, first, second, part, red):
        upper = jnp.sum(first * second, axis=1, keepdims=True)
        lower = jnp.sum(second * second, axis=1, keepdims=True)
        both = jnp.where(lanes == rows, upper, 0.0) + jnp.where(
            lanes == rows + nrhs, lower, 0.0
        )
        row = jnp.sum(both, axis=0, keepdims=True)
        part[...] = row
        red[me] = row

        def send(k, carry):
            red_copy(it, k, part, red).start()
            return carry

        lax.fori_loop(1, count, send, 0)

    def reduce_end(it, part, red):
        def take(k, carry):
            red_copy(it, k, part, red).wait_recv()
            return carry

        lax.fori_loop(1, count, take, 0)
        total = jnp.sum(red[...], axis=0)
        wide = jnp.broadcast_to(total, (nrhs, 128))
        upper = jnp.sum(jnp.where(lanes == rows, wide, 0.0), axis=1, keepdims=True)
        lower = jnp.sum(
            jnp.where(lanes == rows + nrhs, wide, 0.0), axis=1, keepdims=True
        )
        return upper / (lower + 1e-06)

    def to_window(win, source, scale):
        for g in range(leaf_dev):
            block = source[:, g * leaf : (g + 1) * leaf]
            if scale is not None:
                block = block * scale
            win[leaf_dev + g] = block.astype(BF16)

    loads[0].wait()
    to_window(win_a, rhs, None)
    pl.semaphore_wait(barrier, count - 1)
    start_pair(halo_copies(0, win_a))
    for load in loads[1:]:
        load.wait()
    upward(0, win_a, cwin_a, own_a)
    downward(0, cwin_a, own_a)
    recv_pair(halo_copies(0, win_a))
    leaves(0, win_a, image_a, True)

    to_window(win_b, image_a, SHRINK)
    start_pair(halo_copies(1, win_b))
    reduce_start(0, rhs[...], image_a[...], part_a, red_a)
    upward(1, win_b, cwin_b, own_b)
    downward(1, cwin_b, own_b)
    recv_pair(halo_copies(1, win_b))
    leaves(1, win_b, image_b, False)

    alpha = reduce_end(0, part_a, red_a)
    residual = rhs[...] - alpha * image_a[...]
    image = image_a[...] - (alpha * GROW) * image_b[...]
    reduce_start(1, residual, image, part_b, red_b)
    res_ref[...] = residual
    image_b[...] = image

    for it, win, cwins, own, part, red in (
        (0, win_a, cwin_a, own_a, part_a, red_a),
        (1, win_b, cwin_b, own_b, part_b, red_b),
    ):
        sent_pair(halo_copies(it, win))
        for level in range(1, top):
            sent_pair(coef_copies(it, level, cwins[level - 1]))
        for bit in range(bits):
            root_copy(it, bit, own).wait_send()

    beta = reduce_end(1, part_b, red_b)
    sol_ref[...] = alpha * rhs[...] + beta * res_ref[...]
    res_ref[...] = res_ref[...] - beta * image_b[...]

    def drain(k, carry):
        red_copy(0, k, part_a, red_a).wait_send()
        red_copy(1, k, part_b, red_b).wait_send()
        return carry

    lax.fori_loop(1, count, drain, 0)


def body(
    count,
    right_side,
    basis,
    transfer,
    near_tiles,
    near_source,
    near_count,
    couple,
    couple_source,
    couple_count,
    root_couple,
    root_mask,
):
    leaf_dev, rank, leaf = basis.shape
    nrhs = right_side.shape[0]
    sizes = level_sizes(leaf_dev)
    top = len(sizes) - 1
    bits = root_couple.shape[1]
    root_couple = root_couple.reshape(root_couple.shape[1:])
    smem = pl.BlockSpec(memory_space=pltpu.SMEM)
    hbm = pl.BlockSpec(memory_space=pl.ANY)
    vmem = pl.BlockSpec(memory_space=pltpu.VMEM)
    cwins = [pltpu.VMEM((3 * sizes[level], nrhs, rank), BF16) for level in range(1, top)]
    dma = pltpu.SemaphoreType.DMA
    out = jax.ShapeDtypeStruct(right_side.shape, F32)
    return pl.pallas_call(
        functools.partial(kernel, count),
        out_shape=(out, out),
        in_specs=[smem] * 5 + [hbm] * 6,
        out_specs=(vmem, vmem),
        scratch_shapes=[
            pltpu.VMEM(right_side.shape, F32),
            pltpu.VMEM(basis.shape, BF16),
            pltpu.VMEM(transfer.shape, BF16),
            pltpu.VMEM(near_tiles.shape, BF16),
            pltpu.VMEM(couple.shape, BF16),
            pltpu.VMEM(root_couple.shape, BF16),
            pltpu.VMEM(right_side.shape, F32),
            pltpu.VMEM(right_side.shape, F32),
            pltpu.VMEM((leaf_dev, nrhs, rank), BF16),
            pltpu.VMEM((3 * leaf_dev, nrhs, leaf), BF16),
            pltpu.VMEM((3 * leaf_dev, nrhs, leaf), BF16),
            cwins,
            cwins,
            pltpu.VMEM((1 + bits, nrhs, rank), BF16),
            pltpu.VMEM((1 + bits, nrhs, rank), BF16),
            pltpu.VMEM((1, 128), F32),
            pltpu.VMEM((1, 128), F32),
            pltpu.VMEM((count, 1, 128), F32),
            pltpu.VMEM((count, 1, 128), F32),
            dma((5,)),
            dma((leaf_dev,)),
            dma((2, 2)),
            dma((2, 2)),
            dma((2, top - 1, 2)),
            dma((2, top - 1, 2)),
            dma((2, bits)),
            dma((2, bits)),
            dma((2, count)),
            dma((2, count)),
        ],
        compiler_params=pltpu.CompilerParams(
            collective_id=0, has_side_effects=True, vmem_limit_bytes=56 << 20
        ),
        cost_estimate=pl.CostEstimate(
            flops=4 * nrhs * near_tiles.size,
            bytes_accessed=2 * near_tiles.size,
            transcendentals=0,
        ),
    )(
        near_source.T,
        near_count,
        couple_source.T,
        couple_count,
        root_mask,
        right_side,
        basis,
        transfer,
        near_tiles,
        couple,
        root_couple,
    )


def solution(mesh):
    in_specs = (
        P(None, "leaf"),
        P("leaf", None, None),
        P("leaf", None, None),
        P("leaf", None, None, None),
        P("leaf", None),
        P("leaf"),
        P("leaf", None, None, None),
        P("leaf", None),
        P("leaf"),
        P("leaf", None, None, None),
        P("leaf", None),
    )
    out_specs = (P(None, "leaf"), P(None, "leaf"))
    return jax.shard_map(
        functools.partial(body, mesh.shape["leaf"]),
        mesh=mesh,
        in_specs=in_specs,
        out_specs=out_specs,
        check_vma=False,
    )
```

```python
import functools

import jax
import jax.numpy as jnp
from jax import lax
from jax.experimental import pallas as pl
from jax.experimental.pallas import tpu as pltpu
from jax.sharding import PartitionSpec as P

MESH = pl.DeviceIdType.MESH
F32 = jnp.float32
BF16 = jnp.bfloat16
SHRINK = 2.0**-10
GROW = 2.0**10
UNROLL = 4


def dot(a, b):
    return jnp.dot(a, b, preferred_element_type=F32)


def dot_t(a, b):
    return lax.dot_general(a, b, (((1,), (1,)), ((), ())), preferred_element_type=F32)


def level_sizes(leaf_dev):
    sizes = [leaf_dev]
    while sizes[-1] > 1:
        sizes.append(sizes[-1] // 2)
    return sizes


def kernel(
    count,
    near_source_hbm,
    near_count_hbm,
    couple_source_hbm,
    couple_count_hbm,
    root_mask_hbm,
    rhs_hbm,
    basis_hbm,
    transfer_hbm,
    near_hbm,
    couple_hbm,
    root_hbm,
    residual_hbm,
    image_hbm,
    alpha_ref,
    beta_ref,
    near_source,
    near_count,
    couple_source,
    couple_count,
    root_mask,
    rhs,
    basis,
    transfer,
    near,
    couple,
    root,
    image_a,
    image_b,
    residual,
    coupled,
    win_a,
    win_b,
    cwin_a,
    cwin_b,
    own_a,
    own_b,
    part_a,
    part_b,
    red_a,
    red_b,
    load_sem,
    near_sem,
    out_sem,
    halo_send,
    halo_recv,
    coef_send,
    coef_recv,
    root_send,
    root_recv,
    red_send,
    red_recv,
):
    leaf_dev, rank, leaf = basis.shape
    slots = near.shape[1]
    nrhs = rhs.shape[0]
    bits = root.shape[0]
    sizes = level_sizes(leaf_dev)
    top = len(sizes) - 1
    starts = [sum(sizes[:level]) for level in range(top)]
    me = lax.axis_index("leaf")
    has_left = me > 0
    has_right = me < count - 1

    loads = [
        pltpu.make_async_copy(src, dst, load_sem.at[i])
        for i, (src, dst) in enumerate(
            (
                (rhs_hbm, rhs),
                (basis_hbm, basis),
                (transfer_hbm, transfer),
                (couple_hbm, couple),
                (root_hbm, root),
                (near_source_hbm, near_source),
                (near_count_hbm, near_count),
                (couple_source_hbm, couple_source),
                (couple_count_hbm, couple_count),
                (root_mask_hbm, root_mask),
            )
        )
    ]
    for load in loads:
        load.start()

    def near_load(g):
        return pltpu.make_async_copy(near_hbm.at[g], near.at[g], near_sem.at[g])

    barrier = pltpu.get_barrier_semaphore()

    def greet(k, carry):
        pl.semaphore_signal(
            barrier, inc=1, device_id=(lax.rem(me + k, count),), device_id_type=MESH
        )
        return carry

    lax.fori_loop(1, count, greet, 0)

    def halo_copies(it, win):
        own = win.at[pl.ds(leaf_dev, leaf_dev)]
        to_right = pltpu.make_async_remote_copy(
            src_ref=own,
            dst_ref=win.at[pl.ds(0, leaf_dev)],
            send_sem=halo_send.at[it, 0],
            recv_sem=halo_recv.at[it, 0],
            device_id=(me + 1,),
            device_id_type=MESH,
        )
        to_left = pltpu.make_async_remote_copy(
            src_ref=own,
            dst_ref=win.at[pl.ds(2 * leaf_dev, leaf_dev)],
            send_sem=halo_send.at[it, 1],
            recv_sem=halo_recv.at[it, 1],
            device_id=(me - 1,),
            device_id_type=MESH,
        )
        return to_right, to_left

    def coef_copies(it, level, cwin):
        size = sizes[level]
        own = cwin.at[pl.ds(size, size)]
        to_right = pltpu.make_async_remote_copy(
            src_ref=own,
            dst_ref=cwin.at[pl.ds(0, size)],
            send_sem=coef_send.at[it, level - 1, 0],
            recv_sem=coef_recv.at[it, level - 1, 0],
            device_id=(me + 1,),
            device_id_type=MESH,
        )
        to_left = pltpu.make_async_remote_copy(
            src_ref=own,
            dst_ref=cwin.at[pl.ds(2 * size, size)],
            send_sem=coef_send.at[it, level - 1, 1],
            recv_sem=coef_recv.at[it, level - 1, 1],
            device_id=(me - 1,),
            device_id_type=MESH,
        )
        return to_right, to_left

    def start_pair(pair):
        to_right, to_left = pair

        @pl.when(has_right)
        def _():
            to_right.start()

        @pl.when(has_left)
        def _():
            to_left.start()

    def recv_pair(pair):
        to_right, to_left = pair

        @pl.when(has_left)
        def _():
            to_right.wait_recv()

        @pl.when(has_right)
        def _():
            to_left.wait_recv()

    def sent_pair(pair):
        to_right, to_left = pair

        @pl.when(has_right)
        def _():
            to_right.wait_send()

        @pl.when(has_left)
        def _():
            to_left.wait_send()

    def root_copy(it, bit, own):
        step = 1 << bit
        partner = me + step * (1 - 2 * lax.rem(me // step, 2))
        return pltpu.make_async_remote_copy(
            src_ref=own.at[0],
            dst_ref=own.at[1 + bit],
            send_sem=root_send.at[it, bit],
            recv_sem=root_recv.at[it, bit],
            device_id=(partner,),
            device_id_type=MESH,
        )

    def upward(it, win, cwins, own):
        coef = [
            dot_t(win[leaf_dev + g], basis[g]).astype(BF16) for g in range(leaf_dev)
        ]
        for level in range(1, top + 1):
            at = starts[level - 1]
            raised = []
            for j in range(sizes[level]):
                raised.append(
                    (
                        dot(coef[2 * j], transfer[at + 2 * j])
                        + dot(coef[2 * j + 1], transfer[at + 2 * j + 1])
                    ).astype(BF16)
                )
            coef = raised
            if level < top:
                cwin = cwins[level - 1]
                for j in range(sizes[level]):
                    cwin[sizes[level] + j] = coef[j]
                start_pair(coef_copies(it, level, cwin))
        own[0] = coef[0]
        for bit in range(bits):
            root_copy(it, bit, own).start()

    def couplings(it, cwins):
        for level in range(1, top):
            recv_pair(coef_copies(it, level, cwins[level - 1]))
        for level in range(1, top):
            for j in range(sizes[level]):
                row = starts[level] - sizes[0] + j
                live_slots = couple_count[row]
                value = jnp.zeros((nrhs, rank), F32)
                for s in range(couple.shape[1]):
                    index = couple_source[s, row] - (me - 1) * sizes[level]
                    index = jnp.clip(index, 0, 3 * sizes[level] - 1)
                    live = (s < live_slots).astype(F32)
                    value = value + live * dot(cwins[level - 1][index], couple[row, s])
                coupled[row] = value

    def near_field(g, win):
        base = (me - 1) * leaf_dev
        live_slots = near_count[g]
        picked = []
        for s in range(slots):
            live = (s < live_slots).astype(F32).astype(BF16)
            index = jnp.clip(near_source[s, g] - base, 0, 3 * leaf_dev - 1)
            picked.append(win[index] * live)
        x = jnp.concatenate(picked, axis=1)
        return dot(x, near[g].reshape(slots * leaf, leaf))

    def early_leaves(win, image, wait):
        def step(i, carry):
            if wait:
                for u in range(UNROLL):
                    near_load(i * UNROLL + u).wait()
            for u in range(UNROLL):
                g = i * UNROLL + u
                lane = pl.ds(pl.multiple_of(g * leaf, leaf), leaf)
                image[:, lane] = near_field(g, win)
            return carry

        lax.fori_loop(0, leaf_dev // UNROLL - 1, step, 0)

    def late_leaves(it, win, own, image, following, wait):
        last = leaf_dev - UNROLL
        if wait:
            for g in range(last, leaf_dev):
                near_load(g).wait()
        for bit in range(bits):
            root_copy(it, bit, own).wait_recv()
        total = jnp.zeros((nrhs, rank), F32)
        for bit in range(bits):
            total = total + root_mask[0, bit].astype(F32) * dot(own[1 + bit], root[bit])
        field = [total.astype(BF16)]
        for level in range(top - 1, -1, -1):
            down = []
            for j in range(sizes[level]):
                value = dot_t(field[j // 2], transfer[starts[level] + j])
                if level >= 1:
                    value = value + coupled[starts[level] - sizes[0] + j]
                down.append(value.astype(BF16))
            field = down
        late = [near_field(g, win) for g in range(last, leaf_dev)]
        for g in range(leaf_dev):
            lane = slice(g * leaf, (g + 1) * leaf)
            block = image[:, lane] if g < last else late[g - last]
            block = block + dot(field[g], basis[g])
            image[:, lane] = block
            if following is not None:
                following[leaf_dev + g] = (block * SHRINK).astype(BF16)

    rows = lax.broadcasted_iota(jnp.int32, (nrhs, 128), 0)
    lanes = lax.broadcasted_iota(jnp.int32, (nrhs, 128), 1)

    def red_copy(it, k, part, red):
        return pltpu.make_async_remote_copy(
            src_ref=part,
            dst_ref=red.at[me],
            send_sem=red_send.at[it],
            recv_sem=red_recv.at[it],
            device_id=(lax.rem(me + k, count),),
            device_id_type=MESH,
        )

    def every_row(red, sem):
        rows_of_others = red.at[pl.ds(0, count - 1)]
        return pltpu.make_async_copy(rows_of_others, rows_of_others, sem)

    def reduce_start(it, first, second, part, red):
        upper = jnp.sum(first * second, axis=1, keepdims=True)
        lower = jnp.sum(second * second, axis=1, keepdims=True)
        both = jnp.where(lanes == rows, upper, 0.0) + jnp.where(
            lanes == rows + nrhs, lower, 0.0
        )
        row = jnp.sum(both, axis=0, keepdims=True)
        part[...] = row
        red[me] = row

        def send(k, carry):
            red_copy(it, k, part, red).start()
            return carry

        lax.fori_loop(1, count, send, 0)

    def reduce_end(it, part, red):
        every_row(red, red_recv.at[it]).wait()
        total = jnp.sum(red[...], axis=0)
        wide = jnp.broadcast_to(total, (nrhs, 128))
        upper = jnp.sum(jnp.where(lanes == rows, wide, 0.0), axis=1, keepdims=True)
        lower = jnp.sum(
            jnp.where(lanes == rows + nrhs, wide, 0.0), axis=1, keepdims=True
        )
        return upper / (lower + 1e-06)

    loads[0].wait()
    for g in range(leaf_dev):
        win_a[leaf_dev + g] = rhs[:, g * leaf : (g + 1) * leaf].astype(BF16)
    pl.semaphore_wait(barrier, count - 1)
    start_pair(halo_copies(0, win_a))
    for load in loads[1:3]:
        load.wait()
    for g in range(leaf_dev):
        near_load(g).start()
    upward(0, win_a, cwin_a, own_a)
    for load in loads[3:]:
        load.wait()
    couplings(0, cwin_a)
    recv_pair(halo_copies(0, win_a))
    early_leaves(win_a, image_a, True)
    late_leaves(0, win_a, own_a, image_a, win_b, True)

    start_pair(halo_copies(1, win_b))
    reduce_start(0, rhs[...], image_a[...], part_a, red_a)
    upward(1, win_b, cwin_b, own_b)
    couplings(1, cwin_b)
    recv_pair(halo_copies(1, win_b))
    early_leaves(win_b, image_b, False)
    alpha = reduce_end(0, part_a, red_a)
    alpha_ref[...] = jnp.broadcast_to(alpha, alpha_ref.shape)
    residual[...] = rhs[...] - alpha * image_a[...]
    residual_out = pltpu.make_async_copy(residual, residual_hbm, out_sem.at[0])
    residual_out.start()
    late_leaves(1, win_b, own_b, image_b, None, False)

    alpha = alpha_ref[:, :1]
    image_b[...] = image_a[...] - (alpha * GROW) * image_b[...]
    reduce_start(1, residual[...], image_b[...], part_b, red_b)
    image_out = pltpu.make_async_copy(image_b, image_hbm, out_sem.at[1])
    image_out.start()

    for it, win, cwins, own, red in (
        (0, win_a, cwin_a, own_a, red_a),
        (1, win_b, cwin_b, own_b, red_b),
    ):
        sent_pair(halo_copies(it, win))
        for level in range(1, top):
            sent_pair(coef_copies(it, level, cwins[level - 1]))
        for bit in range(bits):
            root_copy(it, bit, own).wait_send()
        every_row(red, red_send.at[it]).wait()
    residual_out.wait()
    image_out.wait()

    beta = reduce_end(1, part_b, red_b)
    beta_ref[...] = jnp.broadcast_to(beta, beta_ref.shape)


def body(
    count,
    right_side,
    basis,
    transfer,
    near_tiles,
    near_source,
    near_count,
    couple,
    couple_source,
    couple_count,
    root_couple,
    root_mask,
):
    leaf_dev, rank, leaf = basis.shape
    nrhs = right_side.shape[0]
    sizes = level_sizes(leaf_dev)
    top = len(sizes) - 1
    bits = root_couple.shape[1]
    root_couple = root_couple.reshape(root_couple.shape[1:])
    hbm = pl.BlockSpec(memory_space=pl.ANY)
    vmem = pl.BlockSpec(memory_space=pltpu.VMEM)
    cwins = [pltpu.VMEM((3 * sizes[level], nrhs, rank), BF16) for level in range(1, top)]
    dma = pltpu.SemaphoreType.DMA
    out = jax.ShapeDtypeStruct(right_side.shape, F32)
    scalar = jax.ShapeDtypeStruct((nrhs, 128), F32)
    residual, image, alpha, beta = pl.pallas_call(
        functools.partial(kernel, count),
        out_shape=(out, out, scalar, scalar),
        in_specs=[hbm] * 11,
        out_specs=(hbm, hbm, vmem, vmem),
        scratch_shapes=[
            pltpu.SMEM(near_source.shape[::-1], jnp.int32),
            pltpu.SMEM(near_count.shape, jnp.int32),
            pltpu.SMEM(couple_source.shape[::-1], jnp.int32),
            pltpu.SMEM(couple_count.shape, jnp.int32),
            pltpu.SMEM(root_mask.shape, jnp.int32),
            pltpu.VMEM(right_side.shape, F32),
            pltpu.VMEM(basis.shape, BF16),
            pltpu.VMEM(transfer.shape, BF16),
            pltpu.VMEM(near_tiles.shape, BF16),
            pltpu.VMEM(couple.shape, BF16),
            pltpu.VMEM(root_couple.shape, BF16),
            pltpu.VMEM(right_side.shape, F32),
            pltpu.VMEM(right_side.shape, F32),
            pltpu.VMEM(right_side.shape, F32),
            pltpu.VMEM((couple.shape[0], nrhs, rank), F32),
            pltpu.VMEM((3 * leaf_dev, nrhs, leaf), BF16),
            pltpu.VMEM((3 * leaf_dev, nrhs, leaf), BF16),
            cwins,
            cwins,
            pltpu.VMEM((1 + bits, nrhs, rank), BF16),
            pltpu.VMEM((1 + bits, nrhs, rank), BF16),
            pltpu.VMEM((1, 128), F32),
            pltpu.VMEM((1, 128), F32),
            pltpu.VMEM((count, 1, 128), F32),
            pltpu.VMEM((count, 1, 128), F32),
            dma((10,)),
            dma((leaf_dev,)),
            dma((2,)),
            dma((2, 2)),
            dma((2, 2)),
            dma((2, top - 1, 2)),
            dma((2, top - 1, 2)),
            dma((2, bits)),
            dma((2, bits)),
            dma((2,)),
            dma((2,)),
        ],
        compiler_params=pltpu.CompilerParams(
            collective_id=0, has_side_effects=True, vmem_limit_bytes=56 << 20
        ),
        cost_estimate=pl.CostEstimate(
            flops=4 * nrhs * near_tiles.size,
            bytes_accessed=2 * near_tiles.size,
            transcendentals=0,
        ),
    )(
        near_source.T,
        near_count,
        couple_source.T,
        couple_count,
        root_mask,
        right_side,
        basis,
        transfer,
        near_tiles,
        couple,
        root_couple,
    )
    alpha, beta = alpha[:, :1], beta[:, :1]
    return (alpha * right_side + beta * residual, residual - beta * image)


def solution(mesh):
    in_specs = (
        P(None, "leaf"),
        P("leaf", None, None),
        P("leaf", None, None),
        P("leaf", None, None, None),
        P("leaf", None),
        P("leaf"),
        P("leaf", None, None, None),
        P("leaf", None),
        P("leaf"),
        P("leaf", None, None, None),
        P("leaf", None),
    )
    out_specs = (P(None, "leaf"), P(None, "leaf"))
    return jax.shard_map(
        functools.partial(body, mesh.shape["leaf"]),
        mesh=mesh,
        in_specs=in_specs,
        out_specs=out_specs,
        check_vma=False,
    )
```

```python
import functools

import jax
import jax.numpy as jnp
from jax import lax
from jax.experimental import pallas as pl
from jax.experimental.pallas import tpu as pltpu
from jax.sharding import PartitionSpec as P

MESH = pl.DeviceIdType.MESH
F32 = jnp.float32
BF16 = jnp.bfloat16
SHRINK = 2.0**-10
GROW = 2.0**10
UNROLL = 8


def dot(a, b):
    return jnp.dot(a, b, preferred_element_type=F32)


def dot_t(a, b):
    return lax.dot_general(a, b, (((1,), (1,)), ((), ())), preferred_element_type=F32)


def level_sizes(leaf_dev):
    sizes = [leaf_dev]
    while sizes[-1] > 1:
        sizes.append(sizes[-1] // 2)
    return sizes


def kernel(
    count,
    near_source_hbm,
    near_count_hbm,
    couple_source_hbm,
    couple_count_hbm,
    root_mask_hbm,
    rhs_hbm,
    basis_hbm,
    transfer_hbm,
    near_hbm,
    couple_hbm,
    root_hbm,
    residual_hbm,
    image_hbm,
    alpha_ref,
    beta_ref,
    near_source,
    near_count,
    couple_source,
    couple_count,
    root_mask,
    rhs,
    basis,
    transfer,
    near,
    couple,
    root,
    image_a,
    image_b,
    residual,
    coupled,
    win_a,
    win_b,
    cwin_a,
    cwin_b,
    own_a,
    own_b,
    part_a,
    part_b,
    red_a,
    red_b,
    load_sem,
    near_sem,
    out_sem,
    halo_send,
    halo_recv,
    coef_send,
    coef_recv,
    root_send,
    root_recv,
    red_send,
    red_recv,
):
    leaf_dev, rank, leaf = basis.shape
    slots = near.shape[1]
    nrhs = rhs.shape[0]
    bits = root.shape[0]
    sizes = level_sizes(leaf_dev)
    top = len(sizes) - 1
    starts = [sum(sizes[:level]) for level in range(top)]
    me = lax.axis_index("leaf")
    has_left = me > 0
    has_right = me < count - 1

    loads = [
        pltpu.make_async_copy(src, dst, load_sem.at[i])
        for i, (src, dst) in enumerate(
            (
                (rhs_hbm, rhs),
                (basis_hbm, basis),
                (transfer_hbm, transfer),
                (couple_hbm, couple),
                (root_hbm, root),
                (near_source_hbm, near_source),
                (near_count_hbm, near_count),
                (couple_source_hbm, couple_source),
                (couple_count_hbm, couple_count),
                (root_mask_hbm, root_mask),
            )
        )
    ]
    for load in loads:
        load.start()

    def near_load(g):
        return pltpu.make_async_copy(near_hbm.at[g], near.at[g], near_sem.at[g])

    barrier = pltpu.get_barrier_semaphore()

    def greet(k, carry):
        pl.semaphore_signal(
            barrier, inc=1, device_id=(lax.rem(me + k, count),), device_id_type=MESH
        )
        return carry

    lax.fori_loop(1, count, greet, 0)

    def halo_copies(it, win):
        own = win.at[pl.ds(leaf_dev, leaf_dev)]
        to_right = pltpu.make_async_remote_copy(
            src_ref=own,
            dst_ref=win.at[pl.ds(0, leaf_dev)],
            send_sem=halo_send.at[it, 0],
            recv_sem=halo_recv.at[it, 0],
            device_id=(me + 1,),
            device_id_type=MESH,
        )
        to_left = pltpu.make_async_remote_copy(
            src_ref=own,
            dst_ref=win.at[pl.ds(2 * leaf_dev, leaf_dev)],
            send_sem=halo_send.at[it, 1],
            recv_sem=halo_recv.at[it, 1],
            device_id=(me - 1,),
            device_id_type=MESH,
        )
        return to_right, to_left

    def coef_copies(it, level, cwin):
        size = sizes[level]
        own = cwin.at[pl.ds(size, size)]
        to_right = pltpu.make_async_remote_copy(
            src_ref=own,
            dst_ref=cwin.at[pl.ds(0, size)],
            send_sem=coef_send.at[it, level - 1, 0],
            recv_sem=coef_recv.at[it, level - 1, 0],
            device_id=(me + 1,),
            device_id_type=MESH,
        )
        to_left = pltpu.make_async_remote_copy(
            src_ref=own,
            dst_ref=cwin.at[pl.ds(2 * size, size)],
            send_sem=coef_send.at[it, level - 1, 1],
            recv_sem=coef_recv.at[it, level - 1, 1],
            device_id=(me - 1,),
            device_id_type=MESH,
        )
        return to_right, to_left

    def start_pair(pair):
        to_right, to_left = pair

        @pl.when(has_right)
        def _():
            to_right.start()

        @pl.when(has_left)
        def _():
            to_left.start()

    def recv_pair(pair):
        to_right, to_left = pair

        @pl.when(has_left)
        def _():
            to_right.wait_recv()

        @pl.when(has_right)
        def _():
            to_left.wait_recv()

    def sent_pair(pair):
        to_right, to_left = pair

        @pl.when(has_right)
        def _():
            to_right.wait_send()

        @pl.when(has_left)
        def _():
            to_left.wait_send()

    def root_copy(it, bit, own):
        step = 1 << bit
        partner = me + step * (1 - 2 * lax.rem(me // step, 2))
        return pltpu.make_async_remote_copy(
            src_ref=own.at[0],
            dst_ref=own.at[1 + bit],
            send_sem=root_send.at[it, bit],
            recv_sem=root_recv.at[it, bit],
            device_id=(partner,),
            device_id_type=MESH,
        )

    def upward(it, win, cwins, own):
        coef = [
            dot_t(win[leaf_dev + g], basis[g]).astype(BF16) for g in range(leaf_dev)
        ]
        for level in range(1, top + 1):
            at = starts[level - 1]
            raised = []
            for j in range(sizes[level]):
                raised.append(
                    (
                        dot(coef[2 * j], transfer[at + 2 * j])
                        + dot(coef[2 * j + 1], transfer[at + 2 * j + 1])
                    ).astype(BF16)
                )
            coef = raised
            if level < top:
                cwin = cwins[level - 1]
                for j in range(sizes[level]):
                    cwin[sizes[level] + j] = coef[j]
                start_pair(coef_copies(it, level, cwin))
        own[0] = coef[0]
        for bit in range(bits):
            root_copy(it, bit, own).start()

    def couplings(it, cwins):
        for level in range(1, top):
            recv_pair(coef_copies(it, level, cwins[level - 1]))
        for level in range(1, top):
            for j in range(sizes[level]):
                row = starts[level] - sizes[0] + j
                live_slots = couple_count[row]
                value = jnp.zeros((nrhs, rank), F32)
                for s in range(couple.shape[1]):
                    index = couple_source[s, row] - (me - 1) * sizes[level]
                    index = jnp.clip(index, 0, 3 * sizes[level] - 1)
                    live = (s < live_slots).astype(F32)
                    value = value + live * dot(cwins[level - 1][index], couple[row, s])
                coupled[row] = value

    def near_field(g, win):
        base = (me - 1) * leaf_dev
        live_slots = near_count[g]
        picked = []
        for s in range(slots):
            live = (s < live_slots).astype(F32).astype(BF16)
            index = jnp.clip(near_source[s, g] - base, 0, 3 * leaf_dev - 1)
            picked.append(win[index] * live)
        x = jnp.concatenate(picked, axis=1)
        return dot(x, near[g].reshape(slots * leaf, leaf))

    def early_leaves(win, image, wait):
        def step(i, carry):
            if wait:
                for u in range(UNROLL):
                    near_load(i * UNROLL + u).wait()
            for u in range(UNROLL):
                g = i * UNROLL + u
                lane = pl.ds(pl.multiple_of(g * leaf, leaf), leaf)
                image[:, lane] = near_field(g, win)
            return carry

        lax.fori_loop(0, leaf_dev // UNROLL - 1, step, 0)

    def late_leaves(it, win, own, image, following, wait):
        last = leaf_dev - UNROLL
        if wait:
            for g in range(last, leaf_dev):
                near_load(g).wait()
        for bit in range(bits):
            root_copy(it, bit, own).wait_recv()
        total = jnp.zeros((nrhs, rank), F32)
        for bit in range(bits):
            total = total + root_mask[0, bit].astype(F32) * dot(own[1 + bit], root[bit])
        field = [total.astype(BF16)]
        for level in range(top - 1, -1, -1):
            down = []
            for j in range(sizes[level]):
                value = dot_t(field[j // 2], transfer[starts[level] + j])
                if level >= 1:
                    value = value + coupled[starts[level] - sizes[0] + j]
                down.append(value.astype(BF16))
            field = down
        late = [near_field(g, win) for g in range(last, leaf_dev)]
        for g in range(leaf_dev):
            lane = slice(g * leaf, (g + 1) * leaf)
            block = image[:, lane] if g < last else late[g - last]
            block = block + dot(field[g], basis[g])
            image[:, lane] = block
            if following is not None:
                following[leaf_dev + g] = (block * SHRINK).astype(BF16)

    rows = lax.broadcasted_iota(jnp.int32, (nrhs, 128), 0)
    lanes = lax.broadcasted_iota(jnp.int32, (nrhs, 128), 1)

    def red_copy(it, k, part, red):
        return pltpu.make_async_remote_copy(
            src_ref=part,
            dst_ref=red.at[me],
            send_sem=red_send.at[it],
            recv_sem=red_recv.at[it],
            device_id=(lax.rem(me + k, count),),
            device_id_type=MESH,
        )

    def every_row(red, sem):
        rows_of_others = red.at[pl.ds(0, count - 1)]
        return pltpu.make_async_copy(rows_of_others, rows_of_others, sem)

    def reduce_start(it, first, second, part, red):
        upper = jnp.sum(first * second, axis=1, keepdims=True)
        lower = jnp.sum(second * second, axis=1, keepdims=True)
        both = jnp.where(lanes == rows, upper, 0.0) + jnp.where(
            lanes == rows + nrhs, lower, 0.0
        )
        row = jnp.sum(both, axis=0, keepdims=True)
        part[...] = row
        red[me] = row

        def send(k, carry):
            red_copy(it, k, part, red).start()
            return carry

        lax.fori_loop(1, count, send, 0)

    def reduce_end(it, part, red):
        every_row(red, red_recv.at[it]).wait()
        total = jnp.sum(red[...], axis=0)
        wide = jnp.broadcast_to(total, (nrhs, 128))
        upper = jnp.sum(jnp.where(lanes == rows, wide, 0.0), axis=1, keepdims=True)
        lower = jnp.sum(
            jnp.where(lanes == rows + nrhs, wide, 0.0), axis=1, keepdims=True
        )
        return upper / (lower + 1e-06)

    loads[0].wait()
    for g in range(leaf_dev):
        win_a[leaf_dev + g] = rhs[:, g * leaf : (g + 1) * leaf].astype(BF16)
    pl.semaphore_wait(barrier, count - 1)
    start_pair(halo_copies(0, win_a))
    for load in loads[1:3]:
        load.wait()
    for g in range(leaf_dev):
        near_load(g).start()
    upward(0, win_a, cwin_a, own_a)
    for load in loads[3:]:
        load.wait()
    couplings(0, cwin_a)
    recv_pair(halo_copies(0, win_a))
    early_leaves(win_a, image_a, True)
    late_leaves(0, win_a, own_a, image_a, win_b, True)

    start_pair(halo_copies(1, win_b))
    reduce_start(0, rhs[...], image_a[...], part_a, red_a)
    upward(1, win_b, cwin_b, own_b)
    couplings(1, cwin_b)
    recv_pair(halo_copies(1, win_b))
    early_leaves(win_b, image_b, False)
    alpha = reduce_end(0, part_a, red_a)
    alpha_ref[...] = jnp.broadcast_to(alpha, alpha_ref.shape)
    residual[...] = rhs[...] - alpha * image_a[...]
    residual_out = pltpu.make_async_copy(residual, residual_hbm, out_sem.at[0])
    residual_out.start()
    late_leaves(1, win_b, own_b, image_b, None, False)

    alpha = alpha_ref[:, :1]
    image_b[...] = image_a[...] - (alpha * GROW) * image_b[...]
    reduce_start(1, residual[...], image_b[...], part_b, red_b)
    image_out = pltpu.make_async_copy(image_b, image_hbm, out_sem.at[1])
    image_out.start()

    for it, win, cwins, own, red in (
        (0, win_a, cwin_a, own_a, red_a),
        (1, win_b, cwin_b, own_b, red_b),
    ):
        sent_pair(halo_copies(it, win))
        for level in range(1, top):
            sent_pair(coef_copies(it, level, cwins[level - 1]))
        for bit in range(bits):
            root_copy(it, bit, own).wait_send()
        every_row(red, red_send.at[it]).wait()
    residual_out.wait()
    image_out.wait()

    beta = reduce_end(1, part_b, red_b)
    beta_ref[...] = jnp.broadcast_to(beta, beta_ref.shape)


def update(alpha, beta, rhs, residual, image, sol_ref, res_ref):
    sol_ref[...] = alpha[:, :1] * rhs[...] + beta[:, :1] * residual[...]
    res_ref[...] = residual[...] - beta[:, :1] * image[...]


def body(
    count,
    right_side,
    basis,
    transfer,
    near_tiles,
    near_source,
    near_count,
    couple,
    couple_source,
    couple_count,
    root_couple,
    root_mask,
):
    leaf_dev, rank, leaf = basis.shape
    nrhs = right_side.shape[0]
    sizes = level_sizes(leaf_dev)
    top = len(sizes) - 1
    bits = root_couple.shape[1]
    root_couple = root_couple.reshape(root_couple.shape[1:])
    hbm = pl.BlockSpec(memory_space=pl.ANY)
    vmem = pl.BlockSpec(memory_space=pltpu.VMEM)
    cwins = [pltpu.VMEM((3 * sizes[level], nrhs, rank), BF16) for level in range(1, top)]
    dma = pltpu.SemaphoreType.DMA
    out = jax.ShapeDtypeStruct(right_side.shape, F32)
    scalar = jax.ShapeDtypeStruct((nrhs, 128), F32)
    residual, image, alpha, beta = pl.pallas_call(
        functools.partial(kernel, count),
        out_shape=(out, out, scalar, scalar),
        in_specs=[hbm] * 11,
        out_specs=(hbm, hbm, vmem, vmem),
        scratch_shapes=[
            pltpu.SMEM(near_source.shape[::-1], jnp.int32),
            pltpu.SMEM(near_count.shape, jnp.int32),
            pltpu.SMEM(couple_source.shape[::-1], jnp.int32),
            pltpu.SMEM(couple_count.shape, jnp.int32),
            pltpu.SMEM(root_mask.shape, jnp.int32),
            pltpu.VMEM(right_side.shape, F32),
            pltpu.VMEM(basis.shape, BF16),
            pltpu.VMEM(transfer.shape, BF16),
            pltpu.VMEM(near_tiles.shape, BF16),
            pltpu.VMEM(couple.shape, BF16),
            pltpu.VMEM(root_couple.shape, BF16),
            pltpu.VMEM(right_side.shape, F32),
            pltpu.VMEM(right_side.shape, F32),
            pltpu.VMEM(right_side.shape, F32),
            pltpu.VMEM((couple.shape[0], nrhs, rank), F32),
            pltpu.VMEM((3 * leaf_dev, nrhs, leaf), BF16),
            pltpu.VMEM((3 * leaf_dev, nrhs, leaf), BF16),
            cwins,
            cwins,
            pltpu.VMEM((1 + bits, nrhs, rank), BF16),
            pltpu.VMEM((1 + bits, nrhs, rank), BF16),
            pltpu.VMEM((1, 128), F32),
            pltpu.VMEM((1, 128), F32),
            pltpu.VMEM((count, 1, 128), F32),
            pltpu.VMEM((count, 1, 128), F32),
            dma((10,)),
            dma((leaf_dev,)),
            dma((2,)),
            dma((2, 2)),
            dma((2, 2)),
            dma((2, top - 1, 2)),
            dma((2, top - 1, 2)),
            dma((2, bits)),
            dma((2, bits)),
            dma((2,)),
            dma((2,)),
        ],
        compiler_params=pltpu.CompilerParams(
            collective_id=0, has_side_effects=True, vmem_limit_bytes=56 << 20
        ),
        cost_estimate=pl.CostEstimate(
            flops=4 * nrhs * near_tiles.size,
            bytes_accessed=2 * near_tiles.size,
            transcendentals=0,
        ),
    )(
        near_source.T,
        near_count,
        couple_source.T,
        couple_count,
        root_mask,
        right_side,
        basis,
        transfer,
        near_tiles,
        couple,
        root_couple,
    )
    return pl.pallas_call(
        update,
        out_shape=(out, out),
        in_specs=[vmem] * 5,
        out_specs=(vmem, vmem),
    )(alpha, beta, right_side, residual, image)


def solution(mesh):
    in_specs = (
        P(None, "leaf"),
        P("leaf", None, None),
        P("leaf", None, None),
        P("leaf", None, None, None),
        P("leaf", None),
        P("leaf"),
        P("leaf", None, None, None),
        P("leaf", None),
        P("leaf"),
        P("leaf", None, None, None),
        P("leaf", None),
    )
    out_specs = (P(None, "leaf"), P(None, "leaf"))
    return jax.shard_map(
        functools.partial(body, mesh.shape["leaf"]),
        mesh=mesh,
        in_specs=in_specs,
        out_specs=out_specs,
        check_vma=False,
    )
```
